32 devices in a mesh: pipe: 2 (over x), expert: 16 (over z, y, core).
Axes of the slice: x: 2, y: 2, z: 4, core: 2. Of those that a mesh axis runs over, the one named last changes fastest.
Arguments:
- down_tokens: bfloat16 [2, 512, 3584], P(None, 'expert'), may hold values from -6 to 6
- up_tokens: bfloat16 [2, 512, 3584], P(None, 'expert'), may hold values from -6 to 6
- norm_gain: float32 [2, 3584], P('pipe'), may hold values from 0.1 to 1.9
- w_gate: bfloat16 [2, 16, 3584, 1024], P('pipe', 'expert'), may hold values from -0.09375 to 0.09375
- w_up: bfloat16 [2, 16, 3584, 1024], P('pipe', 'expert'), may hold values from -0.09375 to 0.09375
- w_down: bfloat16 [2, 16, 1024, 3584], P('pipe', 'expert'), may hold values from -0.1875 to 0.1875
- down_ids: int32 [2, 2, 512, 8], P('pipe', None, 'expert'), may hold values from 0 to 15, all different within a row; in each aligned block of 32 rows (0 to 31, 32 to 63, ..., all dimensions but the last counted through in order) at most 20 rows name the same one
- down_gates: float32 [2, 2, 512, 8], P('pipe', None, 'expert'), may hold values from 0.1 to 1
- up_ids: int32 [2, 2, 512, 8], P('pipe', None, 'expert'), may hold values from 0 to 15, all different within a row; in each aligned block of 32 rows (0 to 31, 32 to 63, ..., all dimensions but the last counted through in order) at most 20 rows name the same one
- up_gates: float32 [2, 2, 512, 8], P('pipe', None, 'expert'), may hold values from 0.1 to 1
- key_cotangent: bfloat16 [2, 2, 2, 512, 64], P('pipe', None, None, 'expert'), may hold values from -0.119628906 to 0.119628906
Outputs:
- down_states: bfloat16 [2, 2, 512, 3584], P('pipe', None, 'expert')
- up_states: bfloat16 [2, 2, 512, 3584], P('pipe', None, 'expert')
- kr_grad: float32 [2, 3584, 64], P('pipe', 'expert')
The draws below stay inside these ranges and needn't reach their ends.
Inputs may be any that keep to these rules, and one draw needn't show every extreme that they name: `down_ids`: each row names 8 different experts. Among the 32 rows of one device in one micro-batch at one section, no expert is named more than 20 times, a bound that some block reaches. `up_ids`: each row names 8 different experts. Among the 32 rows of one device in one micro-batch at one section, no expert is named more than 20 times, a bound that some block reaches.
All inputs are finite; a program needn't handle non-finite values.
Results may differ from the reference program's by a relative error of at most 0.017.
Values may be sent and summed in bfloat16 or wider, within the bound.
A program may use at most 128 MiB of HBM per device.

```python
import math
import jax
import jax.numpy as jnp
import numpy as np
from jax import lax

D = 3584
H = 1024
ROPE = 64
TOP = 8
MB = 2
TOK_DEV = 32
EXPERTS = 16
CAP = 20
TOKENS = 512
N_PIPE = 2
N_EXPERT = 16


def level_of(own_key, shape, cuts, least, largest):
    gain = 1.0
    for dim, parts in cuts:
        heights = jax.random.uniform(jax.random.fold_in(jax.random.fold_in(own_key, 6), dim), (parts,), jnp.float32, least / len(cuts), largest / len(cuts))
        gain = gain * jnp.repeat(jnp.exp(heights), shape[dim] // parts).reshape((-1,) + (1,) * (len(shape) - 1 - dim))
    return gain


def shared_out(rng, own, number, rows, amount, top, bound, slope):
    order = jax.random.permutation(rng, amount)
    heavy_load, ordinary = shares(amount, rows * top, bound, slope, True), shares(amount, rows * top, bound, slope, False)
    places = jnp.arange(amount)

    def named(lengths, offset_by):
        used = int((lengths > 0).sum())
        fixed = max(1, used // 4)
        shifted = fixed + (places - fixed + offset_by * (used - fixed)) % max(1, amount - fixed)
        return jnp.zeros((amount,), jnp.int32).at[order[jnp.where(places < fixed, places, shifted)]].set(jnp.asarray(lengths, jnp.int32))

    lengths = jnp.where(number % 4 == 0, named(heavy_load, number // 4), named(ordinary, number - number // 4 - 1))
    mixed = jax.random.permutation(jax.random.fold_in(own, 3), amount)
    donor, sink = mixed[0:amount // 2 * 2:2], mixed[1:amount // 2 * 2:2]
    room = jnp.minimum(lengths[donor] - 1, bound - lengths[sink]) // 2
    room = jnp.where((donor == order[0]) | (sink == order[0]) | (lengths[sink] == 0), 0, jnp.maximum(room, 0))
    shifted = jax.random.randint(jax.random.fold_in(own, 4), (amount // 2,), 0, 1 << 20) % (room + 1)
    lengths = lengths.at[donor].add(-shifted).at[sink].add(shifted)
    members = jnp.searchsorted(jnp.cumsum(lengths), jnp.arange(rows * top), side="right").astype(jnp.int32)
    listing = members.reshape(top, rows).T
    listing = listing[jax.random.permutation(jax.random.fold_in(own, 1), rows)]
    offset_by = jax.random.randint(jax.random.fold_in(own, 2), (rows, 1), 0, top)
    return jnp.take_along_axis(listing, (jnp.arange(top)[None, :] + offset_by) % top, axis=1)


def shares(number_of, total, limit, skew, full):
    loads = [(1 << 20) // math.isqrt(grade ** skew) + 1 for grade in range(1, number_of + 1)]
    largest = limit if full else min(limit, max(-(-total // number_of), total * loads[0] // sum(loads)))
    least = 1 if total - largest >= number_of - 1 else 0
    given, spare = [largest] + [least] * (number_of - 1), total - largest - least * (number_of - 1)
    while spare > 0:
        movable = [i for i in range(1, number_of) if given[i] < largest] or [i for i in range(1, number_of) if given[i] < limit]
        mass, remaining = sum([loads[i] for i in movable]), spare
        for i in movable:
            addition = min(limit - given[i], max(1, remaining * loads[i] // mass), spare)
            given[i] = given[i] + addition
            spare = spare - addition
    return np.array(given)


def normal_values(stream_key, extent, spread, limit, split=(), kind=jnp.bfloat16):
    entries = jax.random.normal(stream_key, extent, jnp.float32) * spread
    if len(split) > 0:
        entries = level_of(stream_key, extent, split, -0.22, 0.18) * entries
    return jnp.clip(entries, min=-limit, max=limit).astype(kind)


def setup_inputs(seed: int = 0) -> dict:
    streams_of = jax.random.split(jax.random.key(seed), 12)
    down_tokens = normal_values(streams_of[0], (MB, TOKENS, D), 1.0, 6.0, ((1, 16),))
    up_tokens = normal_values(streams_of[1], (MB, TOKENS, D), 1.0, 6.0, ((1, 16),))
    norm_gain = jnp.clip(1.0 + 0.18 * jax.random.normal(streams_of[2], (N_PIPE, D), jnp.float32), 0.1, 1.9)
    w_gate = normal_values(streams_of[3], (N_PIPE, EXPERTS, D, H), D ** -0.5, 0.09375, ((0, 2), (1, 16)))
    w_up = normal_values(streams_of[4], (N_PIPE, EXPERTS, D, H), D ** -0.5, 0.09375, ((0, 2), (1, 16)))
    w_down = normal_values(streams_of[5], (N_PIPE, EXPERTS, H, D), H ** -0.5, 0.1875, ((0, 2), (1, 16)))
    down_ids_keys = jax.random.split(jax.random.fold_in(streams_of[6], 1), N_PIPE * MB * TOKENS // TOK_DEV)
    down_ids_turns = jax.random.permutation(jax.random.fold_in(streams_of[6], 3), N_PIPE * MB * TOKENS // TOK_DEV)
    down_ids = jax.vmap(lambda own, number: shared_out(jax.random.fold_in(streams_of[6], 2), own, number, TOK_DEV, EXPERTS, TOP, CAP, 1))(down_ids_keys, down_ids_turns).reshape((N_PIPE, MB, TOKENS, TOP))
    down_gates = jnp.clip(jnp.exp(math.log(1.0) - 2.3025851 * jax.random.uniform(streams_of[7], (N_PIPE, MB, TOKENS, TOP), jnp.float32) ** level_of(streams_of[7], (N_PIPE, MB, TOKENS, TOP), ((0, 2), (2, 16)), -0.2, 0.2)), 0.1, 1.0)
    up_ids_keys = jax.random.split(jax.random.fold_in(streams_of[8], 1), N_PIPE * MB * TOKENS // TOK_DEV)
    up_ids_turns = jax.random.permutation(jax.random.fold_in(streams_of[8], 3), N_PIPE * MB * TOKENS // TOK_DEV)
    up_ids = jax.vmap(lambda own, number: shared_out(jax.random.fold_in(streams_of[8], 2), own, number, TOK_DEV, EXPERTS, TOP, CAP, 1))(up_ids_keys, up_ids_turns).reshape((N_PIPE, MB, TOKENS, TOP))
    up_gates = jnp.clip(jnp.exp(math.log(1.0) - 2.3025851 * jax.random.uniform(streams_of[9], (N_PIPE, MB, TOKENS, TOP), jnp.float32) ** level_of(streams_of[9], (N_PIPE, MB, TOKENS, TOP), ((0, 2), (2, 16)), -0.2, 0.2)), 0.1, 1.0)
    key_cotangent = normal_values(streams_of[10], (N_PIPE, 2, MB, TOKENS, ROPE), 0.02, 0.119628906, ((0, 2), (3, 16)))
    return {"down_tokens": down_tokens, "up_tokens": up_tokens, "norm_gain": norm_gain, "w_gate": w_gate, "w_up": w_up, "w_down": w_down, "down_ids": down_ids, "down_gates": down_gates, "up_ids": up_ids, "up_gates": up_gates, "key_cotangent": key_cotangent}


EPSILON = 1e-06

def normalize(carried, norm_scale):
    values = carried.astype(jnp.float32)
    inv_rms = lax.rsqrt(lax.optimization_barrier(jnp.mean(values * values, axis=-1, keepdims=True)) + EPSILON)
    return (values * inv_rms * norm_scale).astype(jnp.bfloat16)

def expert_rows(row_block, gate_mat, up_mat, down_mat):
    gate_act = jnp.dot(row_block, gate_mat, preferred_element_type=jnp.float32)
    up_act = jnp.dot(row_block, up_mat, preferred_element_type=jnp.float32)
    hidden = (jax.nn.silu(gate_act) * up_act).astype(jnp.bfloat16)
    return jnp.dot(hidden, down_mat, preferred_element_type=jnp.float32).astype(jnp.bfloat16)

def moe_layer(carried, norm_scale, gate_all, up_all, down_all, route_ids, route_gates):
    normed = normalize(carried, norm_scale)
    flat_ids = route_ids.reshape(-1).astype(jnp.int32)
    flat_gates = route_gates.reshape(-1).astype(jnp.float32)
    row_limit = N_EXPERT * CAP
    positions = jnp.arange(row_limit, dtype=jnp.int32)

    def per_expert(accum, expert):
        matched = flat_ids == expert
        live_count = jnp.sum(matched.astype(jnp.int32))
        pick_index = jnp.nonzero(matched, size=row_limit, fill_value=0)[0].astype(jnp.int32)
        token_index = (pick_index // TOP).astype(jnp.int32)
        outputs = expert_rows(normed[token_index], gate_all[expert], up_all[expert], down_all[expert])
        pick_weight = jnp.where(positions < live_count, flat_gates[pick_index], jnp.zeros_like(flat_gates[pick_index]))
        contrib = pick_weight[:, None] * outputs.astype(jnp.float32)
        return (accum.at[token_index].add(contrib), None)
    accum_start = jnp.zeros(carried.shape, jnp.float32)
    accum, unused = lax.scan(per_expert, accum_start, jnp.arange(EXPERTS, dtype=jnp.int32))
    return ((carried.astype(jnp.float32) + accum).astype(jnp.bfloat16), normed)

def reference(down_tokens, up_tokens, norm_gain, w_gate, w_up, w_down, down_ids, down_gates, up_ids, up_gates, key_cotangent):
    down_rows = [[None] * MB for segment_index in range(N_PIPE)]
    up_rows = [[None] * MB for segment_index in range(N_PIPE)]
    grad_list = [jnp.zeros((D, ROPE), jnp.float32) for segment_index in range(N_PIPE)]
    for micro_index in range(MB):
        carried = down_tokens[micro_index]
        for segment_index in range(N_PIPE):
            carried, normed = moe_layer(carried, norm_gain[segment_index], w_gate[segment_index], w_up[segment_index], w_down[segment_index], down_ids[segment_index, micro_index], down_gates[segment_index, micro_index])
            down_rows[segment_index][micro_index] = carried
            grad_list[segment_index] = grad_list[segment_index] + jnp.dot(normed.T, key_cotangent[segment_index, 0, micro_index], preferred_element_type=jnp.float32)
        carried = up_tokens[micro_index]
        for segment_index in reversed(range(N_PIPE)):
            carried, normed = moe_layer(carried, norm_gain[segment_index], w_gate[segment_index], w_up[segment_index], w_down[segment_index], up_ids[segment_index, micro_index], up_gates[segment_index, micro_index])
            up_rows[segment_index][micro_index] = carried
            grad_list[segment_index] = grad_list[segment_index] + jnp.dot(normed.T, key_cotangent[segment_index, 1, micro_index], preferred_element_type=jnp.float32)
    down_states = jnp.stack([jnp.stack(row_list) for row_list in down_rows])
    up_states = jnp.stack([jnp.stack(row_list) for row_list in up_rows])
    return (down_states, up_states, jnp.stack(grad_list))
```

```python
from functools import partial

import jax
import jax.numpy as jnp
from jax import lax
from jax.experimental import pallas as pl
from jax.experimental.pallas import tpu as pltpu
from jax.sharding import PartitionSpec as P

EPSILON = 1e-06
LANES = 128
MESH = pl.DeviceIdType.MESH


def grid_of(count):
    chips = count // 2
    bits = chips.bit_length() - 1
    far = 1 << ((bits + 1) // 2)
    return far, chips // far


def flipped(value, mask):
    result, bit = value, 1
    while bit <= mask:
        if mask & bit:
            result = result + bit - 2 * bit * ((value // bit) % 2)
        bit *= 2
    return result


def layer_kernel(
    count, far, near, window,
    x_ref, carried_ref, gate_hbm, up_hbm, down_hbm,
    out_ref, kr_ref,
    rows, w_gate, w_up, w_down, hidden, core_in, near_in, far_in,
    w_sem, z_send, y_send, c_send, ag_recv,
    rc_send, rc_recv, ry_send, ry_recv, rz_send, rz_recv,
):
    micro, tokens, width = x_ref.shape
    features, units = w_gate.shape
    lane_rows = near * far * tokens
    me = lax.axis_index("expert")
    pipe = lax.axis_index("pipe")
    c = me % 2
    y = (me // 2) % near
    z = me // (2 * near)

    def device(cc, yy, zz):
        return (pipe, (zz * near + yy) * 2 + cc)

    def slot(cc, yy, zz):
        return (cc * near + yy) * far + zz

    def span(cc, yy, zz):
        return pl.ds(pl.multiple_of(slot(cc, yy, zz) * tokens, tokens), tokens)

    def lane_span(cc):
        return pl.ds(pl.multiple_of(cc * lane_rows, lane_rows), lane_rows)

    core_peer = device(1 - c, y, z)
    near_peers = {k: device(c, flipped(y, k), z) for k in range(1, near)}
    far_peers = {k: device(c, y, flipped(z, k)) for k in range(1, far)}
    partners = [core_peer] + list(near_peers.values()) + list(far_peers.values())

    loads = [
        pltpu.make_async_copy(gate_hbm, w_gate, w_sem.at[0]),
        pltpu.make_async_copy(up_hbm, w_up, w_sem.at[1]),
        pltpu.make_async_copy(down_hbm, w_down, w_sem.at[2]),
    ]
    for load in loads:
        load.start()

    barrier = pltpu.get_barrier_semaphore()
    for partner in partners:
        pl.semaphore_signal(barrier, inc=1, device_id=partner, device_id_type=MESH)
    pl.semaphore_wait(barrier, len(partners))

    kr_ref[...] = jnp.zeros_like(kr_ref)
    window_start = jnp.minimum(me * (features // count) // LANES * LANES, width - window)

    def move(m, cc, yy, zz, send_sem, target):
        where = rows.at[m, span(cc, yy, zz)]
        return pltpu.make_async_remote_copy(
            src_ref=where, dst_ref=where, send_sem=send_sem,
            recv_sem=ag_recv.at[m, slot(cc, yy, zz)], device_id=target, device_id_type=MESH,
        )

    def arrived(m, cc, yy, zz):
        move(m, cc, yy, zz, z_send.at[m, 0], core_peer).wait_recv()

    sends = [[] for _ in range(micro)]

    def start(m, copy):
        copy.start()
        sends[m].append(copy)

    def to_near(m, k):
        zz = flipped(z, k)
        for j in range(1, near):
            start(m, move(m, c, y, zz, y_send.at[m, j * far + k], near_peers[j]))

    def to_core(m, j, k):
        start(m, move(m, c, flipped(y, j), flipped(z, k), c_send.at[m, j * far + k], core_peer))

    def gather_start(m):
        rows[m, span(c, y, z)] = x_ref[m]
        for k in range(1, far):
            start(m, move(m, c, y, z, z_send.at[m, k], far_peers[k]))
        to_near(m, 0)
        to_core(m, 0, 0)

    def gather_far(m):
        for k in range(1, far):
            arrived(m, c, y, flipped(z, k))
            to_near(m, k)
            to_core(m, 0, k)

    def gather_near(m):
        for k in range(far):
            for j in range(1, near):
                arrived(m, c, flipped(y, j), flipped(z, k))
                to_core(m, j, k)

    def gather_core(m):
        for k in range(far):
            for j in range(near):
                arrived(m, 1 - c, flipped(y, j), flipped(z, k))
        for copy in sends[m]:
            copy.wait_send()

    unit_tile = 256 if units % 256 == 0 else units
    feature_tile = 512 if features % 512 == 0 else features

    def expand(m, cc):
        here = lane_span(cc)
        kr_ref[...] += lax.dot_general(
            rows[m, here, pl.ds(features, width - features)],
            rows[m, here, pl.ds(pl.multiple_of(window_start, LANES), window)],
            (((0,), (0,)), ((), ())), preferred_element_type=jnp.float32,
        )

        def body(i, carry):
            tile = pl.ds(pl.multiple_of(i * unit_tile, unit_tile), unit_tile)
            block = rows[m, here, pl.ds(0, features)]
            gate = jnp.dot(block, w_gate[:, tile], preferred_element_type=jnp.float32)
            up = jnp.dot(block, w_up[:, tile], preferred_element_type=jnp.float32)
            hidden[:, tile] = (gate / (1.0 + jnp.exp(-gate)) * up).astype(jnp.bfloat16)
            return carry

        lax.fori_loop(0, units // unit_tile, body, 0)

    def contract(m, cc, add):
        here = lane_span(cc)
        extra = rows[m, here, pl.ds(features, width - features)].astype(jnp.float32)
        lane = lax.broadcasted_iota(jnp.int32, extra.shape, 1)
        mine = (lane == me) | (lane == count + me)
        weight = jnp.sum(jnp.where(mine, extra, 0.0), axis=1, keepdims=True)

        def body(i, carry):
            tile = pl.ds(pl.multiple_of(i * feature_tile, feature_tile), feature_tile)
            part = jnp.dot(hidden[...], w_down[:, tile], preferred_element_type=jnp.float32) * weight
            if add:
                part = part + core_in[m, :, tile].astype(jnp.float32)
            rows[m, here, tile] = part.astype(jnp.bfloat16)
            return carry

        lax.fori_loop(0, features // feature_tile, body, 0)

    columns = pl.ds(0, features)

    def core_sum(m):
        return pltpu.make_async_remote_copy(
            src_ref=rows.at[m, lane_span(1 - c), columns], dst_ref=core_in.at[m],
            send_sem=rc_send.at[m], recv_sem=rc_recv.at[m],
            device_id=core_peer, device_id_type=MESH,
        )

    def near_sum(m, j, k):
        zz = flipped(z, k)
        return pltpu.make_async_remote_copy(
            src_ref=rows.at[m, span(c, flipped(y, j), zz), columns],
            dst_ref=near_in.at[m, j - 1, zz],
            send_sem=ry_send.at[m, j - 1, zz], recv_sem=ry_recv.at[m, j - 1, zz],
            device_id=near_peers[j], device_id_type=MESH,
        )

    def far_sum(m, k):
        return pltpu.make_async_remote_copy(
            src_ref=rows.at[m, span(c, y, flipped(z, k)), columns],
            dst_ref=far_in.at[m, k - 1],
            send_sem=rz_send.at[m, k - 1], recv_sem=rz_recv.at[m, k - 1],
            device_id=far_peers[k], device_id_type=MESH,
        )

    far_order = list(range(far - 1, -1, -1))

    def near_start(m):
        for k in far_order:
            for j in range(1, near):
                near_sum(m, j, k).start()

    def near_finish(m):
        for k in far_order:
            here = span(c, y, flipped(z, k))
            total = rows[m, here, columns].astype(jnp.float32)
            for j in range(1, near):
                near_sum(m, j, k).wait_recv()
                total = total + near_in[m, j - 1, flipped(z, k)].astype(jnp.float32)
            rows[m, here, columns] = total.astype(jnp.bfloat16)
            if k > 0:
                far_sum(m, k).start()

    def far_finish(m):
        total = carried_ref[m].astype(jnp.float32) + rows[m, span(c, y, z), columns].astype(jnp.float32)
        for k in range(1, far):
            far_sum(m, k).wait_recv()
            total = total + far_in[m, k - 1].astype(jnp.float32)
        out_ref[m] = total.astype(jnp.bfloat16)

    gather_start(0)
    gather_far(0)
    for m in range(micro):
        later, before = m + 1 < micro, m > 0
        if later:
            gather_start(m + 1)
        if m == 0:
            gather_near(0)
        gather_core(m)
        if m == 0:
            loads[0].wait()
            loads[1].wait()
        expand(m, 1 - c)
        if later:
            gather_far(m + 1)
        if before:
            near_finish(m - 1)
        if m == 0:
            loads[2].wait()
        contract(m, 1 - c, False)
        core_sum(m).start()
        expand(m, c)
        if later:
            gather_near(m + 1)
        if before:
            far_finish(m - 1)
        core_sum(m).wait_recv()
        contract(m, c, True)
        near_start(m)
    near_finish(micro - 1)
    far_finish(micro - 1)
    for m in range(micro):
        core_sum(m).wait_send()
        for k in range(far):
            for j in range(1, near):
                near_sum(m, j, k).wait_send()
            if k > 0:
                far_sum(m, k).wait_send()


def run_layer(x, carried, w_gate, w_up, w_down, count):
    far, near = grid_of(count)
    micro, tokens, width = x.shape
    features, units = w_gate.shape
    lane_rows = near * far * tokens
    share = features // count
    window = -(-(share + LANES - 1) // LANES) * LANES
    bf16 = jnp.bfloat16
    dma = pltpu.SemaphoreType.DMA
    total_rows = 2 * lane_rows * micro
    return pl.pallas_call(
        partial(layer_kernel, count, far, near, window),
        out_shape=(
            jax.ShapeDtypeStruct(carried.shape, bf16),
            jax.ShapeDtypeStruct((width - features, window), jnp.float32),
        ),
        in_specs=[pl.BlockSpec(memory_space=pltpu.VMEM)] * 2 + [pl.BlockSpec(memory_space=pl.ANY)] * 3,
        out_specs=(pl.BlockSpec(memory_space=pltpu.VMEM),) * 2,
        scratch_shapes=[
            pltpu.VMEM((micro, 2 * lane_rows, width), bf16),
            pltpu.VMEM(w_gate.shape, bf16),
            pltpu.VMEM(w_up.shape, bf16),
            pltpu.VMEM(w_down.shape, bf16),
            pltpu.VMEM((lane_rows, units), bf16),
            pltpu.VMEM((micro, lane_rows, features), bf16),
            pltpu.VMEM((micro, near - 1, far, tokens, features), bf16),
            pltpu.VMEM((micro, far - 1, tokens, features), bf16),
            dma((3,)),
            dma((micro, far)),
            dma((micro, near * far)),
            dma((micro, near * far)),
            dma((micro, count)),
            dma((micro,)),
            dma((micro,)),
            dma((micro, near - 1, far)),
            dma((micro, near - 1, far)),
            dma((micro, far - 1)),
            dma((micro, far - 1)),
        ],
        compiler_params=pltpu.CompilerParams(
            collective_id=0, has_side_effects=True, vmem_limit_bytes=60 * 1024 * 1024
        ),
        cost_estimate=pl.CostEstimate(
            flops=6 * total_rows * features * units,
            bytes_accessed=6 * features * units,
            transcendentals=total_rows * units,
        ),
    )(x, carried, w_gate, w_up, w_down)


def normalize(carried, norm_scale):
    values = carried.astype(jnp.float32)
    inv_rms = lax.rsqrt(jnp.mean(values * values, axis=-1, keepdims=True) + EPSILON)
    return (values * inv_rms * norm_scale).astype(jnp.bfloat16)


def side_columns(ids, gates, tangents, count, width):
    named = (ids[..., None] == jnp.arange(count, dtype=jnp.int32)).astype(jnp.float32)
    weight = jnp.sum(gates[..., None] * named, axis=-2)
    high = weight.astype(jnp.bfloat16)
    low = (weight - high.astype(jnp.float32)).astype(jnp.bfloat16)
    side = jnp.concatenate([high, low, tangents], axis=-1)
    return jnp.pad(side, ((0, 0), (0, 0), (0, width - side.shape[-1])))


def on_device(
    down_tokens,
    up_tokens,
    norm_gain,
    w_gate,
    w_up,
    w_down,
    down_ids,
    down_gates,
    up_ids,
    up_gates,
    key_cotangent,
):
    sections = lax.axis_size("pipe")
    section = lax.axis_index("pipe")
    count = lax.axis_size("expert")
    features = down_tokens.shape[-1]
    rope = key_cotangent.shape[-1]
    share = features // count
    side_width = -(-(2 * count + rope) // LANES) * LANES
    window = -(-(share + LANES - 1) // LANES) * LANES
    side_down = side_columns(down_ids[0], down_gates[0], key_cotangent[0, 0], count, side_width)
    side_up = side_columns(up_ids[0], up_gates[0], key_cotangent[0, 1], count, side_width)
    carried = jnp.where(section == 0, down_tokens, up_tokens)
    down_states = jnp.zeros_like(down_tokens)
    up_states = jnp.zeros_like(up_tokens)
    key_grad = 0.0
    for turn in range(sections):
        down_on = section == turn
        up_on = section == sections - 1 - turn
        side = jnp.where(down_on, side_down, side_up)
        side = jnp.where(down_on | up_on, side, jnp.zeros_like(side))
        x = jnp.concatenate([normalize(carried, norm_gain[0]), side], axis=-1)
        output, grad = run_layer(x, carried, w_gate[0, 0], w_up[0, 0], w_down[0, 0], count)
        key_grad = key_grad + grad
        down_states = jnp.where(down_on, output, down_states)
        up_states = jnp.where(up_on, output, up_states)
        if turn + 1 < sections:
            carried = lax.ppermute(
                output, "pipe", [(turn, turn + 1), (sections - 1 - turn, sections - 2 - turn)]
            )
    first = lax.axis_index("expert") * share
    start = jnp.minimum(first // LANES * LANES, features + side_width - window)
    grad_rows = lax.dynamic_slice(key_grad, (2 * count, first - start), (rope, share)).T
    return (down_states[None], up_states[None], grad_rows[None])


def solution(mesh):
    return jax.shard_map(
        on_device,
        mesh=mesh,
        in_specs=(
            P(None, "expert", None),
            P(None, "expert", None),
            P("pipe", None),
            P("pipe", "expert", None, None),
            P("pipe", "expert", None, None),
            P("pipe", "expert", None, None),
            P("pipe", None, "expert", None),
            P("pipe", None, "expert", None),
            P("pipe", None, "expert", None),
            P("pipe", None, "expert", None),
            P("pipe", None, None, "expert", None),
        ),
        out_specs=(
            P("pipe", None, "expert", None),
            P("pipe", None, "expert", None),
            P("pipe", "expert", None),
        ),
        check_vma=False,
    )
```

```python
from functools import partial

import jax
import jax.numpy as jnp
from jax import lax
from jax.experimental import pallas as pl
from jax.experimental.pallas import tpu as pltpu
from jax.sharding import PartitionSpec as P

EPSILON = 1e-06
LANES = 128
MESH = pl.DeviceIdType.MESH


def grid_of(count):
    chips = count // 2
    bits = chips.bit_length() - 1
    far = 1 << ((bits + 1) // 2)
    return far, chips // far


def flipped(value, mask):
    result, bit = value, 1
    while bit <= mask:
        if mask & bit:
            result = result + bit - 2 * bit * ((value // bit) % 2)
        bit *= 2
    return result


def layer_kernel(
    count, far, near, window,
    x_ref, carried_ref, gate_hbm, up_hbm, down_hbm,
    out_ref, kr_ref,
    rows, w_gate, w_up, w_down, hidden, core_in, near_in, far_in,
    w_sem, z_send, y_send, c_send, ag_recv,
    rc_send, rc_recv, ry_send, ry_recv, rz_send, rz_recv,
):
    micro, tokens, width = x_ref.shape
    features, units = w_gate.shape
    lane_rows = near * far * tokens
    me = lax.axis_index("expert")
    pipe = lax.axis_index("pipe")
    c = me % 2
    y = (me // 2) % near
    z = me // (2 * near)

    def device(cc, yy, zz):
        return (pipe, (zz * near + yy) * 2 + cc)

    def slot(cc, yy, zz):
        return (cc * near + yy) * far + zz

    def span(cc, yy, zz):
        return pl.ds(pl.multiple_of(slot(cc, yy, zz) * tokens, tokens), tokens)

    def lane_span(cc):
        return pl.ds(pl.multiple_of(cc * lane_rows, lane_rows), lane_rows)

    core_peer = device(1 - c, y, z)
    near_peers = {k: device(c, flipped(y, k), z) for k in range(1, near)}
    far_peers = {k: device(c, y, flipped(z, k)) for k in range(1, far)}
    partners = [core_peer] + list(near_peers.values()) + list(far_peers.values())

    loads = [
        pltpu.make_async_copy(gate_hbm, w_gate, w_sem.at[0]),
        pltpu.make_async_copy(up_hbm, w_up, w_sem.at[1]),
        pltpu.make_async_copy(down_hbm, w_down, w_sem.at[2]),
    ]
    for load in loads:
        load.start()

    barrier = pltpu.get_barrier_semaphore()
    for partner in partners:
        pl.semaphore_signal(barrier, inc=1, device_id=partner, device_id_type=MESH)
    pl.semaphore_wait(barrier, len(partners))

    kr_ref[...] = jnp.zeros_like(kr_ref)
    window_start = jnp.minimum(me * (features // count) // LANES * LANES, width - window)

    def move(m, cc, yy, zz, send_sem, target):
        where = rows.at[m, span(cc, yy, zz)]
        return pltpu.make_async_remote_copy(
            src_ref=where, dst_ref=where, send_sem=send_sem,
            recv_sem=ag_recv.at[m, slot(cc, yy, zz)], device_id=target, device_id_type=MESH,
        )

    def arrived(m, cc, yy, zz):
        move(m, cc, yy, zz, z_send.at[m, 0], core_peer).wait_recv()

    def to_near(m, zz):
        return [move(m, c, y, zz, y_send.at[m, j * far + zz], near_peers[j]) for j in range(1, near)]

    def to_core(m, j, zz):
        return move(m, c, flipped(y, j), zz, c_send.at[m, j * far + zz], core_peer)

    def along(m, side, hop):
        held = z - side * (hop - 1)
        there = (held >= 0) & (held < far) & (z + side >= 0) & (z + side < far)
        return there, move(m, c, y, held, z_send.at[m, (side + 1) // 2 * far + hop], device(c, y, z + side))

    def gather_start(m):
        rows[m, span(c, y, z)] = x_ref[m]
        for side in (1, -1):
            there, copy = along(m, side, 1)
            pl.when(there)(copy.start)
        for copy in to_near(m, z):
            copy.start()
        to_core(m, 0, z).start()

    def gather_far(m, hop):
        for side in (1, -1):
            zz = z - side * hop

            @pl.when((zz >= 0) & (zz < far))
            def _():
                arrived(m, c, y, zz)
                for copy in to_near(m, zz):
                    copy.start()
                if hop + 1 < far:
                    there, copy = along(m, side, hop + 1)
                    pl.when(there)(copy.start)
                to_core(m, 0, zz).start()

    def gather_near(m, hop):
        for side in (1, -1)[: 2 if hop else 1]:
            zz = z - side * hop

            @pl.when((zz >= 0) & (zz < far))
            def _():
                for j in range(1, near):
                    arrived(m, c, flipped(y, j), zz)
                    to_core(m, j, zz).start()

    def gather_core(m):
        for yy in range(near):
            for zz in range(far):
                arrived(m, 1 - c, yy, zz)
        for side in (1, -1):
            for hop in range(1, far):
                there, copy = along(m, side, hop)
                pl.when(there)(copy.wait_send)
        for zz in range(far):
            for copy in to_near(m, zz):
                copy.wait_send()
            for j in range(near):
                to_core(m, j, zz).wait_send()

    unit_tile = 256 if units % 256 == 0 else units
    feature_tile = 512 if features % 512 == 0 else features

    def key_product(m, cc):
        here = lane_span(cc)
        kr_ref[...] += lax.dot_general(
            rows[m, here, pl.ds(features, width - features)],
            rows[m, here, pl.ds(pl.multiple_of(window_start, LANES), window)],
            (((0,), (0,)), ((), ())), preferred_element_type=jnp.float32,
        )

    def expand(m, cc, first, last):
        here = lane_span(cc)

        def body(i, carry):
            tile = pl.ds(pl.multiple_of(i * unit_tile, unit_tile), unit_tile)
            block = rows[m, here, pl.ds(0, features)]
            gate = jnp.dot(block, w_gate[:, tile], preferred_element_type=jnp.float32)
            up = jnp.dot(block, w_up[:, tile], preferred_element_type=jnp.float32)
            hidden[:, tile] = (gate / (1.0 + jnp.exp(-gate)) * up).astype(jnp.bfloat16)
            return carry

        lax.fori_loop(first, last, body, 0)

    def contract(m, cc, add):
        here = lane_span(cc)
        extra = rows[m, here, pl.ds(features, width - features)].astype(jnp.float32)
        lane = lax.broadcasted_iota(jnp.int32, extra.shape, 1)
        mine = (lane == me) | (lane == count + me)
        weight = jnp.sum(jnp.where(mine, extra, 0.0), axis=1, keepdims=True)

        def body(i, carry):
            tile = pl.ds(pl.multiple_of(i * feature_tile, feature_tile), feature_tile)
            part = jnp.dot(hidden[...], w_down[:, tile], preferred_element_type=jnp.float32) * weight
            if add:
                part = part + core_in[m, :, tile].astype(jnp.float32)
            rows[m, here, tile] = part.astype(jnp.bfloat16)
            return carry

        lax.fori_loop(0, features // feature_tile, body, 0)

    columns = pl.ds(0, features)

    def core_sum(m):
        return pltpu.make_async_remote_copy(
            src_ref=rows.at[m, lane_span(1 - c), columns], dst_ref=core_in.at[m],
            send_sem=rc_send.at[m], recv_sem=rc_recv.at[m],
            device_id=core_peer, device_id_type=MESH,
        )

    def near_sum(m, j, k):
        zz = flipped(z, k)
        return pltpu.make_async_remote_copy(
            src_ref=rows.at[m, span(c, flipped(y, j), zz), columns],
            dst_ref=near_in.at[m, j - 1, zz],
            send_sem=ry_send.at[m, j - 1, zz], recv_sem=ry_recv.at[m, j - 1, zz],
            device_id=near_peers[j], device_id_type=MESH,
        )

    def far_sum(m, k):
        return pltpu.make_async_remote_copy(
            src_ref=rows.at[m, span(c, y, flipped(z, k)), columns],
            dst_ref=far_in.at[m, k - 1],
            send_sem=rz_send.at[m, k - 1], recv_sem=rz_recv.at[m, k - 1],
            device_id=far_peers[k], device_id_type=MESH,
        )

    far_order = list(range(far - 1, -1, -1))

    def near_start(m):
        for k in far_order:
            for j in range(1, near):
                near_sum(m, j, k).start()

    def near_finish(m, k):
        here = span(c, y, flipped(z, k))
        total = rows[m, here, columns].astype(jnp.float32)
        for j in range(1, near):
            near_sum(m, j, k).wait_recv()
            total = total + near_in[m, j - 1, flipped(z, k)].astype(jnp.float32)
        rows[m, here, columns] = total.astype(jnp.bfloat16)
        if k > 0:
            far_sum(m, k).start()

    def far_finish(m):
        total = carried_ref[m].astype(jnp.float32) + rows[m, span(c, y, z), columns].astype(jnp.float32)
        for k in range(1, far):
            far_sum(m, k).wait_recv()
            total = total + far_in[m, k - 1].astype(jnp.float32)
        out_ref[m] = total.astype(jnp.bfloat16)

    tiles = units // unit_tile
    gather_start(0)
    for hop in range(1, far):
        gather_far(0, hop)
        gather_near(0, hop - 1)
    if micro > 1:
        gather_start(1)
    gather_near(0, far - 1)
    for m in range(micro):
        later, before = m + 1 < micro, m > 0
        if later and before:
            gather_start(m + 1)
        gather_core(m)
        ahead = []
        if later:
            for hop in range(1, far):
                ahead.append([partial(gather_far, m + 1, hop), partial(gather_near, m + 1, hop - 1)])
            ahead.append([partial(gather_near, m + 1, far - 1)])
        behind = [[partial(near_finish, m - 1, k)] for k in far_order] if before else []
        queues = [queue for queue in (ahead, behind) if queue]

        def advance(most=1):
            for queue in queues:
                for _ in range(min(most, len(queue))):
                    for piece in queue.pop(0):
                        piece()

        if m == 0:
            loads[0].wait()
            loads[1].wait()
        expand(m, 1 - c, 0, tiles // 2)
        if later:
            advance()
        expand(m, 1 - c, tiles // 2, tiles)
        key_product(m, 1 - c)
        if not later:
            advance()
        if m == 0:
            loads[2].wait()
        contract(m, 1 - c, False)
        core_sum(m).start()
        advance()
        expand(m, c, 0, tiles // 2)
        if later:
            advance()
        expand(m, c, tiles // 2, tiles)
        key_product(m, c)
        if not later:
            advance()
        core_sum(m).wait_recv()
        contract(m, c, True)
        near_start(m)
        advance(far)
        if before:
            far_finish(m - 1)
    for k in far_order:
        near_finish(micro - 1, k)
    far_finish(micro - 1)
    for m in range(micro):
        core_sum(m).wait_send()
        for k in range(far):
            for j in range(1, near):
                near_sum(m, j, k).wait_send()
            if k > 0:
                far_sum(m, k).wait_send()


def run_layer(x, carried, w_gate, w_up, w_down, count):
    far, near = grid_of(count)
    micro, tokens, width = x.shape
    features, units = w_gate.shape
    lane_rows = near * far * tokens
    share = features // count
    window = -(-(share + LANES - 1) // LANES) * LANES
    bf16 = jnp.bfloat16
    dma = pltpu.SemaphoreType.DMA
    total_rows = 2 * lane_rows * micro
    return pl.pallas_call(
        partial(layer_kernel, count, far, near, window),
        out_shape=(
            jax.ShapeDtypeStruct(carried.shape, bf16),
            jax.ShapeDtypeStruct((width - features, window), jnp.float32),
        ),
        in_specs=[pl.BlockSpec(memory_space=pltpu.VMEM)] * 2 + [pl.BlockSpec(memory_space=pl.ANY)] * 3,
        out_specs=(pl.BlockSpec(memory_space=pltpu.VMEM),) * 2,
        scratch_shapes=[
            pltpu.VMEM((micro, 2 * lane_rows, width), bf16),
            pltpu.VMEM(w_gate.shape, bf16),
            pltpu.VMEM(w_up.shape, bf16),
            pltpu.VMEM(w_down.shape, bf16),
            pltpu.VMEM((lane_rows, units), bf16),
            pltpu.VMEM((micro, lane_rows, features), bf16),
            pltpu.VMEM((micro, near - 1, far, tokens, features), bf16),
            pltpu.VMEM((micro, far - 1, tokens, features), bf16),
            dma((3,)),
            dma((micro, 2 * far)),
            dma((micro, near * far)),
            dma((micro, near * far)),
            dma((micro, count)),
            dma((micro,)),
            dma((micro,)),
            dma((micro, near - 1, far)),
            dma((micro, near - 1, far)),
            dma((micro, far - 1)),
            dma((micro, far - 1)),
        ],
        compiler_params=pltpu.CompilerParams(
            collective_id=0, has_side_effects=True, vmem_limit_bytes=60 * 1024 * 1024
        ),
        cost_estimate=pl.CostEstimate(
            flops=6 * total_rows * features * units,
            bytes_accessed=6 * features * units,
            transcendentals=total_rows * units,
        ),
    )(x, carried, w_gate, w_up, w_down)


def normalize(carried, norm_scale):
    values = carried.astype(jnp.float32)
    inv_rms = lax.rsqrt(jnp.mean(values * values, axis=-1, keepdims=True) + EPSILON)
    return (values * inv_rms * norm_scale).astype(jnp.bfloat16)


def side_columns(ids, gates, tangents, count, width):
    named = (ids[..., None] == jnp.arange(count, dtype=jnp.int32)).astype(jnp.float32)
    weight = jnp.sum(gates[..., None] * named, axis=-2)
    high = weight.astype(jnp.bfloat16)
    low = (weight - high.astype(jnp.float32)).astype(jnp.bfloat16)
    side = jnp.concatenate([high, low, tangents], axis=-1)
    return jnp.pad(side, ((0, 0), (0, 0), (0, width - side.shape[-1])))


def on_device(
    down_tokens,
    up_tokens,
    norm_gain,
    w_gate,
    w_up,
    w_down,
    down_ids,
    down_gates,
    up_ids,
    up_gates,
    key_cotangent,
):
    sections = lax.axis_size("pipe")
    section = lax.axis_index("pipe")
    count = lax.axis_size("expert")
    features = down_tokens.shape[-1]
    rope = key_cotangent.shape[-1]
    share = features // count
    side_width = -(-(2 * count + rope) // LANES) * LANES
    window = -(-(share + LANES - 1) // LANES) * LANES
    side_down = side_columns(down_ids[0], down_gates[0], key_cotangent[0, 0], count, side_width)
    side_up = side_columns(up_ids[0], up_gates[0], key_cotangent[0, 1], count, side_width)
    carried = jnp.where(section == 0, down_tokens, up_tokens)
    down_states = jnp.zeros_like(down_tokens)
    up_states = jnp.zeros_like(up_tokens)
    key_grad = 0.0
    for turn in range(sections):
        down_on = section == turn
        up_on = section == sections - 1 - turn
        side = jnp.where(down_on, side_down, side_up)
        side = jnp.where(down_on | up_on, side, jnp.zeros_like(side))
        x = jnp.concatenate([normalize(carried, norm_gain[0]), side], axis=-1)
        output, grad = run_layer(x, carried, w_gate[0, 0], w_up[0, 0], w_down[0, 0], count)
        key_grad = key_grad + grad
        down_states = jnp.where(down_on, output, down_states)
        up_states = jnp.where(up_on, output, up_states)
        if turn + 1 < sections:
            carried = lax.ppermute(
                output, "pipe", [(turn, turn + 1), (sections - 1 - turn, sections - 2 - turn)]
            )
    first = lax.axis_index("expert") * share
    start = jnp.minimum(first // LANES * LANES, features + side_width - window)
    grad_rows = lax.dynamic_slice(key_grad, (2 * count, first - start), (rope, share)).T
    return (down_states[None], up_states[None], grad_rows[None])


def solution(mesh):
    return jax.shard_map(
        on_device,
        mesh=mesh,
        in_specs=(
            P(None, "expert", None),
            P(None, "expert", None),
            P("pipe", None),
            P("pipe", "expert", None, None),
            P("pipe", "expert", None, None),
            P("pipe", "expert", None, None),
            P("pipe", None, "expert", None),
            P("pipe", None, "expert", None),
            P("pipe", None, "expert", None),
            P("pipe", None, "expert", None),
            P("pipe", None, None, "expert", None),
        ),
        out_specs=(
            P("pipe", None, "expert", None),
            P("pipe", None, "expert", None),
            P("pipe", "expert", None),
        ),
        check_vma=False,
    )
```

```python
from functools import partial

import jax
import jax.numpy as jnp
from jax import lax
from jax.experimental import pallas as pl
from jax.experimental.pallas import tpu as pltpu
from jax.sharding import PartitionSpec as P

EPSILON = 1e-06
LANES = 128
MESH = pl.DeviceIdType.MESH


def grid_of(count):
    chips = count // 2
    bits = chips.bit_length() - 1
    far = 1 << ((bits + 1) // 2)
    return far, chips // far


def flipped(value, mask):
    result, bit = value, 1
    while bit <= mask:
        if mask & bit:
            result = result + bit - 2 * bit * ((value // bit) % 2)
        bit *= 2
    return result


def layer_kernel(
    count, far, near, window, turns,
    tokens_ref, side_ref, gain_ref, gate_hbm, up_hbm, down_hbm,
    out_ref, kr_ref,
    rows, passed, w_gate, w_up, w_down, hidden, core_in, near_in, far_in,
    w_sem, z_send, y_send, c_send, ag_recv,
    rc_send, rc_recv, ry_send, ry_recv, rz_send, rz_recv, p_send, p_recv,
):
    micro, tokens, _ = tokens_ref.shape
    width = rows.shape[2]
    features, units = w_gate.shape
    lane_rows = near * far * tokens
    me = lax.axis_index("expert")
    pipe = lax.axis_index("pipe")
    c = me % 2
    y = (me // 2) % near
    z = me // (2 * near)

    def device(cc, yy, zz):
        return (pipe, (zz * near + yy) * 2 + cc)

    def slot(cc, yy, zz):
        return (cc * near + yy) * far + zz

    def span(cc, yy, zz):
        return pl.ds(pl.multiple_of(slot(cc, yy, zz) * tokens, tokens), tokens)

    def lane_span(cc):
        return pl.ds(pl.multiple_of(cc * lane_rows, lane_rows), lane_rows)

    core_peer = device(1 - c, y, z)
    near_peers = {k: device(c, flipped(y, k), z) for k in range(1, near)}
    far_peers = {k: device(c, y, flipped(z, k)) for k in range(1, far)}
    partners = [core_peer] + list(near_peers.values()) + list(far_peers.values())
    if turns > 1:
        partners.append((1 - pipe, me))

    loads = [
        pltpu.make_async_copy(gate_hbm, w_gate, w_sem.at[0]),
        pltpu.make_async_copy(up_hbm, w_up, w_sem.at[1]),
        pltpu.make_async_copy(down_hbm, w_down, w_sem.at[2]),
    ]
    for load in loads:
        load.start()

    barrier = pltpu.get_barrier_semaphore()
    for partner in partners:
        pl.semaphore_signal(barrier, inc=1, device_id=partner, device_id_type=MESH)
    pl.semaphore_wait(barrier, len(partners))

    kr_ref[...] = jnp.zeros_like(kr_ref)
    window_start = jnp.minimum(me * (features // count) // LANES * LANES, width - window)

    def move(m, cc, yy, zz, send_sem, target):
        where = rows.at[m, span(cc, yy, zz)]
        return pltpu.make_async_remote_copy(
            src_ref=where, dst_ref=where, send_sem=send_sem,
            recv_sem=ag_recv.at[m, slot(cc, yy, zz)], device_id=target, device_id_type=MESH,
        )

    def arrived(m, cc, yy, zz):
        move(m, cc, yy, zz, z_send.at[m, 0], core_peer).wait_recv()

    def to_near(m, zz):
        return [move(m, c, y, zz, y_send.at[m, j * far + zz], near_peers[j]) for j in range(1, near)]

    def to_core(m, j, zz):
        return move(m, c, flipped(y, j), zz, c_send.at[m, j * far + zz], core_peer)

    def along(m, side, hop):
        held = z - side * (hop - 1)
        there = (held >= 0) & (held < far) & (z + side >= 0) & (z + side < far)
        return there, move(m, c, y, held, z_send.at[m, (side + 1) // 2 * far + hop], device(c, y, z + side))

    def pass_on(m):
        return pltpu.make_async_remote_copy(
            src_ref=out_ref.at[m], dst_ref=passed.at[m], send_sem=p_send.at[m],
            recv_sem=p_recv.at[m], device_id=(1 - pipe, me), device_id_type=MESH,
        )

    def carried(m):
        value = tokens_ref[m] if m < micro else passed[m - micro]
        return value.astype(jnp.float32)

    def gather_start(m):
        if m >= micro:
            pass_on(m - micro).wait_recv()
        values = carried(m)
        inv_rms = lax.rsqrt(jnp.mean(values * values, axis=-1, keepdims=True) + EPSILON)
        rows[m, span(c, y, z), pl.ds(0, features)] = (values * inv_rms * gain_ref[...]).astype(jnp.bfloat16)
        rows[m, span(c, y, z), pl.ds(features, width - features)] = side_ref[m]
        for side in (1, -1):
            there, copy = along(m, side, 1)
            pl.when(there)(copy.start)
        for copy in to_near(m, z):
            copy.start()
        to_core(m, 0, z).start()

    def gather_far(m, hop):
        for side in (1, -1):
            zz = z - side * hop

            @pl.when((zz >= 0) & (zz < far))
            def _():
                arrived(m, c, y, zz)
                for copy in to_near(m, zz):
                    copy.start()
                if hop + 1 < far:
                    there, copy = along(m, side, hop + 1)
                    pl.when(there)(copy.start)
                to_core(m, 0, zz).start()

    def gather_near(m, hop):
        for side in (1, -1)[: 2 if hop else 1]:
            zz = z - side * hop

            @pl.when((zz >= 0) & (zz < far))
            def _():
                for j in range(1, near):
                    arrived(m, c, flipped(y, j), zz)
                    to_core(m, j, zz).start()

    def gather_core(m):
        for yy in range(near):
            for zz in range(far):
                arrived(m, 1 - c, yy, zz)
        for side in (1, -1):
            for hop in range(1, far):
                there, copy = along(m, side, hop)
                pl.when(there)(copy.wait_send)
        for zz in range(far):
            for copy in to_near(m, zz):
                copy.wait_send()
            for j in range(near):
                to_core(m, j, zz).wait_send()

    unit_tile = 256 if units % 256 == 0 else units
    feature_tile = 512 if features % 512 == 0 else features

    def key_product(m, cc):
        here = lane_span(cc)
        kr_ref[...] += lax.dot_general(
            rows[m, here, pl.ds(features, width - features)],
            rows[m, here, pl.ds(pl.multiple_of(window_start, LANES), window)],
            (((0,), (0,)), ((), ())), preferred_element_type=jnp.float32,
        )

    def expand(m, cc, first, last):
        here = lane_span(cc)

        def body(i, carry):
            tile = pl.ds(pl.multiple_of(i * unit_tile, unit_tile), unit_tile)
            block = rows[m, here, pl.ds(0, features)]
            gate = jnp.dot(block, w_gate[:, tile], preferred_element_type=jnp.float32)
            up = jnp.dot(block, w_up[:, tile], preferred_element_type=jnp.float32)
            hidden[:, tile] = (gate / (1.0 + jnp.exp(-gate)) * up).astype(jnp.bfloat16)
            return carry

        lax.fori_loop(first, last, body, 0)

    def contract(m, cc, add):
        here = lane_span(cc)
        extra = rows[m, here, pl.ds(features, width - features)].astype(jnp.float32)
        lane = lax.broadcasted_iota(jnp.int32, extra.shape, 1)
        mine = (lane == me) | (lane == count + me)
        weight = jnp.sum(jnp.where(mine, extra, 0.0), axis=1, keepdims=True)

        def body(i, carry):
            tile = pl.ds(pl.multiple_of(i * feature_tile, feature_tile), feature_tile)
            part = jnp.dot(hidden[...], w_down[:, tile], preferred_element_type=jnp.float32) * weight
            if add:
                part = part + core_in[m, :, tile].astype(jnp.float32)
            rows[m, here, tile] = part.astype(jnp.bfloat16)
            return carry

        lax.fori_loop(0, features // feature_tile, body, 0)

    columns = pl.ds(0, features)

    def core_sum(m):
        return pltpu.make_async_remote_copy(
            src_ref=rows.at[m, lane_span(1 - c), columns], dst_ref=core_in.at[m],
            send_sem=rc_send.at[m], recv_sem=rc_recv.at[m],
            device_id=core_peer, device_id_type=MESH,
        )

    def near_sum(m, j, k):
        zz = flipped(z, k)
        return pltpu.make_async_remote_copy(
            src_ref=rows.at[m, span(c, flipped(y, j), zz), columns],
            dst_ref=near_in.at[m, j - 1, zz],
            send_sem=ry_send.at[m, j - 1, zz], recv_sem=ry_recv.at[m, j - 1, zz],
            device_id=near_peers[j], device_id_type=MESH,
        )

    def far_sum(m, k):
        return pltpu.make_async_remote_copy(
            src_ref=rows.at[m, span(c, y, flipped(z, k)), columns],
            dst_ref=far_in.at[m, k - 1],
            send_sem=rz_send.at[m, k - 1], recv_sem=rz_recv.at[m, k - 1],
            device_id=far_peers[k], device_id_type=MESH,
        )

    far_order = list(range(far - 1, -1, -1))

    def near_start(m):
        for k in far_order:
            for j in range(1, near):
                near_sum(m, j, k).start()

    def near_finish(m, k):
        here = span(c, y, flipped(z, k))
        total = rows[m, here, columns].astype(jnp.float32)
        for j in range(1, near):
            near_sum(m, j, k).wait_recv()
            total = total + near_in[m, j - 1, flipped(z, k)].astype(jnp.float32)
        rows[m, here, columns] = total.astype(jnp.bfloat16)
        if k > 0:
            far_sum(m, k).start()

    def far_finish(m):
        total = carried(m) + rows[m, span(c, y, z), columns].astype(jnp.float32)
        for k in range(1, far):
            far_sum(m, k).wait_recv()
            total = total + far_in[m, k - 1].astype(jnp.float32)
        out_ref[m] = total.astype(jnp.bfloat16)
        if m < (turns - 1) * micro:
            pass_on(m).start()

    tiles = units // unit_tile
    tiles = units // unit_tile
    items = turns * micro
    gather_start(0)
    for hop in range(1, far):
        gather_far(0, hop)
        gather_near(0, hop - 1)
    if micro > 1:
        gather_start(1)
    gather_near(0, far - 1)
    for m in range(items):
        later, before = (m + 1) % micro > 0, m % micro > 0
        if later and before:
            gather_start(m + 1)
        gather_core(m)
        ahead = []
        if later:
            if m >= micro and not before:
                ahead.append([partial(gather_start, m + 1)])
            for hop in range(1, far):
                ahead.append([partial(gather_far, m + 1, hop), partial(gather_near, m + 1, hop - 1)])
            ahead.append([partial(gather_near, m + 1, far - 1)])
        behind = [[partial(near_finish, m - 1, k)] for k in far_order] if before else []
        queues = [queue for queue in (ahead, behind) if queue]

        def advance(most=1):
            for queue in queues:
                for _ in range(min(most, len(queue))):
                    for piece in queue.pop(0):
                        piece()

        if m == 0:
            loads[0].wait()
            loads[1].wait()
        expand(m, 1 - c, 0, tiles // 2)
        if later:
            advance()
        expand(m, 1 - c, tiles // 2, tiles)
        key_product(m, 1 - c)
        if not later:
            advance()
        if m == 0:
            loads[2].wait()
        contract(m, 1 - c, False)
        core_sum(m).start()
        advance()
        expand(m, c, 0, tiles // 2)
        if later:
            advance()
        expand(m, c, tiles // 2, tiles)
        key_product(m, c)
        if not later:
            advance()
        core_sum(m).wait_recv()
        contract(m, c, True)
        near_start(m)
        advance(far + 1)
        if before:
            far_finish(m - 1)
        if later:
            continue
        more = m + 1 < items
        if more:
            gather_start(m + 1)
        for step, k in enumerate(far_order):
            near_finish(m, k)
            if more and step > 0:
                gather_far(m + 1, step)
                gather_near(m + 1, step - 1)
        far_finish(m)
        if more:
            gather_near(m + 1, far - 1)
    for m in range(items - micro):
        pass_on(m).wait_send()
    for m in range(items):
        core_sum(m).wait_send()
        for k in range(far):
            for j in range(1, near):
                near_sum(m, j, k).wait_send()
            if k > 0:
                far_sum(m, k).wait_send()


def run_layer(tokens_in, side, gain, w_gate, w_up, w_down, count):
    far, near = grid_of(count)
    micro, tokens, features = tokens_in.shape
    items, _, side_width = side.shape
    units = w_gate.shape[1]
    width = features + side_width
    lane_rows = near * far * tokens
    share = features // count
    window = -(-(share + LANES - 1) // LANES) * LANES
    bf16 = jnp.bfloat16
    dma = pltpu.SemaphoreType.DMA
    total_rows = 2 * lane_rows * items
    return pl.pallas_call(
        partial(layer_kernel, count, far, near, window, items // micro),
        out_shape=(
            jax.ShapeDtypeStruct((items, tokens, features), bf16),
            jax.ShapeDtypeStruct((side_width, window), jnp.float32),
        ),
        in_specs=[pl.BlockSpec(memory_space=pltpu.VMEM)] * 3 + [pl.BlockSpec(memory_space=pl.ANY)] * 3,
        out_specs=(pl.BlockSpec(memory_space=pltpu.VMEM),) * 2,
        scratch_shapes=[
            pltpu.VMEM((items, 2 * lane_rows, width), bf16),
            pltpu.VMEM(tokens_in.shape, bf16),
            pltpu.VMEM(w_gate.shape, bf16),
            pltpu.VMEM(w_up.shape, bf16),
            pltpu.VMEM(w_down.shape, bf16),
            pltpu.VMEM((lane_rows, units), bf16),
            pltpu.VMEM((items, lane_rows, features), bf16),
            pltpu.VMEM((items, near - 1, far, tokens, features), bf16),
            pltpu.VMEM((items, far - 1, tokens, features), bf16),
            dma((3,)),
            dma((items, 2 * far)),
            dma((items, near * far)),
            dma((items, near * far)),
            dma((items, count)),
            dma((items,)),
            dma((items,)),
            dma((items, near - 1, far)),
            dma((items, near - 1, far)),
            dma((items, far - 1)),
            dma((items, far - 1)),
            dma((micro,)),
            dma((micro,)),
        ],
        compiler_params=pltpu.CompilerParams(
            collective_id=0, has_side_effects=True, vmem_limit_bytes=60 * 1024 * 1024
        ),
        cost_estimate=pl.CostEstimate(
            flops=6 * total_rows * features * units,
            bytes_accessed=6 * features * units,
            transcendentals=total_rows * units,
        ),
    )(tokens_in, side, gain, w_gate, w_up, w_down)


def side_columns(ids, gates, tangents, count, width):
    named = (ids[..., None] == jnp.arange(count, dtype=jnp.int32)).astype(jnp.float32)
    weight = jnp.sum(gates[..., None] * named, axis=-2)
    high = weight.astype(jnp.bfloat16)
    low = (weight - high.astype(jnp.float32)).astype(jnp.bfloat16)
    side = jnp.concatenate([high, low, tangents], axis=-1)
    return jnp.pad(side, ((0, 0), (0, 0), (0, width - side.shape[-1])))


def on_device(
    down_tokens,
    up_tokens,
    norm_gain,
    w_gate,
    w_up,
    w_down,
    down_ids,
    down_gates,
    up_ids,
    up_gates,
    key_cotangent,
):
    sections = lax.axis_size("pipe")
    section = lax.axis_index("pipe")
    count = lax.axis_size("expert")
    features = down_tokens.shape[-1]
    rope = key_cotangent.shape[-1]
    share = features // count
    side_width = -(-(2 * count + rope) // LANES) * LANES
    window = -(-(share + LANES - 1) // LANES) * LANES
    side_down = side_columns(down_ids[0], down_gates[0], key_cotangent[0, 0], count, side_width)
    side_up = side_columns(up_ids[0], up_gates[0], key_cotangent[0, 1], count, side_width)
    carried = jnp.where(section == 0, down_tokens, up_tokens)
    down_states = jnp.zeros_like(down_tokens)
    up_states = jnp.zeros_like(up_tokens)
    key_grad = 0.0
    micro = down_tokens.shape[0]
    turns = sections if sections == 2 and micro > 1 else 1
    for call in range(0, sections, turns):
        sides = []
        for turn in range(call, call + turns):
            down_on, up_on = section == turn, section == sections - 1 - turn
            side = jnp.where(down_on, side_down, side_up)
            sides.append(jnp.where(down_on | up_on, side, jnp.zeros_like(side)))
        side = jnp.concatenate(sides, axis=0)
        outputs, grad = run_layer(carried, side, norm_gain, w_gate[0, 0], w_up[0, 0], w_down[0, 0], count)
        key_grad = key_grad + grad
        for turn in range(call, call + turns):
            output = outputs[(turn - call) * micro : (turn - call + 1) * micro]
            down_states = jnp.where(section == turn, output, down_states)
            up_states = jnp.where(section == sections - 1 - turn, output, up_states)
        if turn + 1 < sections:
            carried = lax.ppermute(
                output, "pipe", [(turn, turn + 1), (sections - 1 - turn, sections - 2 - turn)]
            )
    first = lax.axis_index("expert") * share
    start = jnp.minimum(first // LANES * LANES, features + side_width - window)
    grad_rows = lax.dynamic_slice(key_grad, (2 * count, first - start), (rope, share)).T
    return (down_states[None], up_states[None], grad_rows[None])


def solution(mesh):
    return jax.shard_map(
        on_device,
        mesh=mesh,
        in_specs=(
            P(None, "expert", None),
            P(None, "expert", None),
            P("pipe", None),
            P("pipe", "expert", None, None),
            P("pipe", "expert", None, None),
            P("pipe", "expert", None, None),
            P("pipe", None, "expert", None),
            P("pipe", None, "expert", None),
            P("pipe", None, "expert", None),
            P("pipe", None, "expert", None),
            P("pipe", None, None, "expert", None),
        ),
        out_specs=(
            P("pipe", None, "expert", None),
            P("pipe", None, "expert", None),
            P("pipe", "expert", None),
        ),
        check_vma=False,
    )
```

```python
from functools import partial

import jax
import jax.numpy as jnp
from jax import lax
from jax.experimental import pallas as pl
from jax.experimental.pallas import tpu as pltpu
from jax.sharding import PartitionSpec as P

EPSILON = 1e-06
LANES = 128
MESH = pl.DeviceIdType.MESH


def grid_of(count):
    chips = count // 2
    bits = chips.bit_length() - 1
    far = 1 << ((bits + 1) // 2)
    return far, chips // far


def flipped(value, mask):
    result, bit = value, 1
    while bit <= mask:
        if mask & bit:
            result = result + bit - 2 * bit * ((value // bit) % 2)
        bit *= 2
    return result


def layer_kernel(
    count, far, near, window, turns,
    tokens_ref, side_ref, gain_ref, gate_hbm, up_hbm, down_hbm,
    out_ref, kr_ref,
    rows, passed, w_gate, w_up, w_down, hidden, core_in, near_in, far_in,
    w_sem, z_send, y_send, c_send, ag_recv,
    rc_send, rc_recv, ry_send, ry_recv, rz_send, rz_recv, p_send, p_recv,
):
    micro, tokens, _ = tokens_ref.shape
    width = rows.shape[2]
    features, units = w_gate.shape
    lane_rows = near * far * tokens
    me = lax.axis_index("expert")
    pipe = lax.axis_index("pipe")
    c = me % 2
    y = (me // 2) % near
    z = me // (2 * near)

    def device(cc, yy, zz):
        return (pipe, (zz * near + yy) * 2 + cc)

    def slot(cc, yy, zz):
        return (cc * near + yy) * far + zz

    def span(cc, yy, zz):
        return pl.ds(pl.multiple_of(slot(cc, yy, zz) * tokens, tokens), tokens)

    def lane_span(cc):
        return pl.ds(pl.multiple_of(cc * lane_rows, lane_rows), lane_rows)

    core_peer = device(1 - c, y, z)
    near_peers = {k: device(c, flipped(y, k), z) for k in range(1, near)}
    far_peers = {k: device(c, y, flipped(z, k)) for k in range(1, far)}
    partners = [core_peer] + list(near_peers.values()) + list(far_peers.values())
    if turns > 1:
        partners.append((1 - pipe, me))

    loads = [
        pltpu.make_async_copy(gate_hbm, w_gate, w_sem.at[0]),
        pltpu.make_async_copy(up_hbm, w_up, w_sem.at[1]),
        pltpu.make_async_copy(down_hbm, w_down, w_sem.at[2]),
    ]
    for load in loads:
        load.start()

    barrier = pltpu.get_barrier_semaphore()
    for partner in partners:
        pl.semaphore_signal(barrier, inc=1, device_id=partner, device_id_type=MESH)
    pl.semaphore_wait(barrier, len(partners))

    kr_ref[...] = jnp.zeros_like(kr_ref)
    window_start = jnp.minimum(me * (features // count) // LANES * LANES, width - window)

    def move(m, cc, yy, zz, send_sem, target):
        where = rows.at[m, span(cc, yy, zz)]
        return pltpu.make_async_remote_copy(
            src_ref=where, dst_ref=where, send_sem=send_sem,
            recv_sem=ag_recv.at[m, slot(cc, yy, zz)], device_id=target, device_id_type=MESH,
        )

    def arrived(m, cc, yy, zz):
        move(m, cc, yy, zz, z_send.at[m, 0], core_peer).wait_recv()

    def to_near(m, zz):
        return [move(m, c, y, zz, y_send.at[m, j * far + zz], near_peers[j]) for j in range(1, near)]

    def to_core(m, j, zz):
        return move(m, c, flipped(y, j), zz, c_send.at[m, j * far + zz], core_peer)

    def along(m, side, hop):
        held = z - side * (hop - 1)
        there = (held >= 0) & (held < far) & (z + side >= 0) & (z + side < far)
        return there, move(m, c, y, held, z_send.at[m, (side + 1) // 2 * far + hop], device(c, y, z + side))

    def pass_on(m):
        return pltpu.make_async_remote_copy(
            src_ref=out_ref.at[m], dst_ref=passed.at[m], send_sem=p_send.at[m],
            recv_sem=p_recv.at[m], device_id=(1 - pipe, me), device_id_type=MESH,
        )

    def carried(m):
        value = tokens_ref[m] if m < micro else passed[m - micro]
        return value.astype(jnp.float32)

    def gather_start(m):
        if m >= micro:
            pass_on(m - micro).wait_recv()
        values = carried(m)
        inv_rms = lax.rsqrt(jnp.mean(values * values, axis=-1, keepdims=True) + EPSILON)
        rows[m, span(c, y, z), pl.ds(0, features)] = (values * inv_rms * gain_ref[...]).astype(jnp.bfloat16)
        rows[m, span(c, y, z), pl.ds(features, width - features)] = side_ref[m]
        for side in (1, -1):
            there, copy = along(m, side, 1)
            pl.when(there)(copy.start)
        for copy in to_near(m, z):
            copy.start()
        to_core(m, 0, z).start()

    def gather_far(m, hop):
        for side in (1, -1):
            zz = z - side * hop

            @pl.when((zz >= 0) & (zz < far))
            def _():
                arrived(m, c, y, zz)
                for copy in to_near(m, zz):
                    copy.start()
                if hop + 1 < far:
                    there, copy = along(m, side, hop + 1)
                    pl.when(there)(copy.start)
                to_core(m, 0, zz).start()

    def gather_near(m, hop):
        for side in (1, -1)[: 2 if hop else 1]:
            zz = z - side * hop

            @pl.when((zz >= 0) & (zz < far))
            def _():
                for j in range(1, near):
                    arrived(m, c, flipped(y, j), zz)
                    to_core(m, j, zz).start()

    def gather_core(m):
        for yy in range(near):
            for zz in range(far):
                arrived(m, 1 - c, yy, zz)
        for side in (1, -1):
            for hop in range(1, far):
                there, copy = along(m, side, hop)
                pl.when(there)(copy.wait_send)
        for zz in range(far):
            for copy in to_near(m, zz):
                copy.wait_send()
            for j in range(near):
                to_core(m, j, zz).wait_send()

    unit_tile = 256 if units % 256 == 0 else units
    feature_tile = 512 if features % 512 == 0 else features

    def key_product(m, cc):
        here = lane_span(cc)
        kr_ref[...] += lax.dot_general(
            rows[m, here, pl.ds(features, width - features)],
            rows[m, here, pl.ds(pl.multiple_of(window_start, LANES), window)],
            (((0,), (0,)), ((), ())), preferred_element_type=jnp.float32,
        )

    def expand(m, cc, first, last):
        here = lane_span(cc)

        def body(i, carry):
            tile = pl.ds(pl.multiple_of(i * unit_tile, unit_tile), unit_tile)
            block = rows[m, here, pl.ds(0, features)]
            gate = jnp.dot(block, w_gate[:, tile], preferred_element_type=jnp.float32)
            up = jnp.dot(block, w_up[:, tile], preferred_element_type=jnp.float32)
            hidden[:, tile] = (gate / (1.0 + jnp.exp(-gate)) * up).astype(jnp.bfloat16)
            return carry

        lax.fori_loop(first, last, body, 0)

    def contract(m, cc, add):
        here = lane_span(cc)
        extra = rows[m, here, pl.ds(features, width - features)].astype(jnp.float32)
        lane = lax.broadcasted_iota(jnp.int32, extra.shape, 1)
        mine = (lane == me) | (lane == count + me)
        weight = jnp.sum(jnp.where(mine, extra, 0.0), axis=1, keepdims=True)

        def body(i, carry):
            tile = pl.ds(pl.multiple_of(i * feature_tile, feature_tile), feature_tile)
            part = jnp.dot(hidden[...], w_down[:, tile], preferred_element_type=jnp.float32) * weight
            if add:
                part = part + core_in[m, :, tile].astype(jnp.float32)
            rows[m, here, tile] = part.astype(jnp.bfloat16)
            return carry

        lax.fori_loop(0, features // feature_tile, body, 0)

    columns = pl.ds(0, features)

    def core_sum(m):
        return pltpu.make_async_remote_copy(
            src_ref=rows.at[m, lane_span(1 - c), columns], dst_ref=core_in.at[m],
            send_sem=rc_send.at[m], recv_sem=rc_recv.at[m],
            device_id=core_peer, device_id_type=MESH,
        )

    def near_sum(m, j, k):
        zz = flipped(z, k)
        return pltpu.make_async_remote_copy(
            src_ref=rows.at[m, span(c, flipped(y, j), zz), columns],
            dst_ref=near_in.at[m, j - 1, zz],
            send_sem=ry_send.at[m, j - 1, zz], recv_sem=ry_recv.at[m, j - 1, zz],
            device_id=near_peers[j], device_id_type=MESH,
        )

    def far_sum(m, k):
        return pltpu.make_async_remote_copy(
            src_ref=rows.at[m, span(c, y, flipped(z, k)), columns],
            dst_ref=far_in.at[m, k - 1],
            send_sem=rz_send.at[m, k - 1], recv_sem=rz_recv.at[m, k - 1],
            device_id=far_peers[k], device_id_type=MESH,
        )

    far_order = list(range(far - 1, -1, -1))

    def near_start(m):
        for k in far_order:
            for j in range(1, near):
                near_sum(m, j, k).start()

    def near_finish(m, k):
        here = span(c, y, flipped(z, k))
        total = rows[m, here, columns].astype(jnp.float32)
        for j in range(1, near):
            near_sum(m, j, k).wait_recv()
            total = total + near_in[m, j - 1, flipped(z, k)].astype(jnp.float32)
        rows[m, here, columns] = total.astype(jnp.bfloat16)
        if k > 0:
            far_sum(m, k).start()

    def far_finish(m):
        total = carried(m) + rows[m, span(c, y, z), columns].astype(jnp.float32)
        for k in range(1, far):
            far_sum(m, k).wait_recv()
            total = total + far_in[m, k - 1].astype(jnp.float32)
        out_ref[m] = total.astype(jnp.bfloat16)
        if m < (turns - 1) * micro:
            pass_on(m).start()

    tiles = units // unit_tile
    tiles = units // unit_tile
    items = turns * micro
    gather_start(0)
    for hop in range(1, far):
        gather_far(0, hop)
        gather_near(0, hop - 1)
    if micro > 1:
        gather_start(1)
    gather_near(0, far - 1)
    for m in range(items):
        later, before = (m + 1) % micro > 0, m % micro > 0
        if later and before:
            gather_start(m + 1)
        gather_core(m)
        ahead = []
        if later:
            if m >= micro and not before:
                ahead.append([partial(gather_start, m + 1)])
            for hop in range(1, far):
                ahead.append([partial(gather_far, m + 1, hop), partial(gather_near, m + 1, hop - 1)])
            ahead.append([partial(gather_near, m + 1, far - 1)])
        behind = [[partial(near_finish, m - 1, k)] for k in far_order] if before else []
        queues = [queue for queue in (ahead, behind) if queue]

        def advance(most=1):
            for queue in queues:
                for _ in range(min(most, len(queue))):
                    for piece in queue.pop(0):
                        piece()

        if m == 0:
            loads[0].wait()
            loads[1].wait()
        expand(m, 1 - c, 0, tiles // 2)
        if later:
            advance()
        expand(m, 1 - c, tiles // 2, tiles)
        key_product(m, 1 - c)
        if not later:
            advance()
        if m == 0:
            loads[2].wait()
        contract(m, 1 - c, False)
        core_sum(m).start()
        advance()
        expand(m, c, 0, tiles // 2)
        if later:
            advance()
        expand(m, c, tiles // 2, tiles)
        key_product(m, c)
        if not later:
            advance()
        core_sum(m).wait_recv()
        contract(m, c, True)
        near_start(m)
        advance(far + 1)
        if before:
            far_finish(m - 1)
        if later:
            continue
        more = m + 1 < items
        for step, k in enumerate(far_order):
            near_finish(m, k)
            if more and step == 0:
                gather_start(m + 1)
            if more and step > 0:
                gather_far(m + 1, step)
                gather_near(m + 1, step - 1)
        far_finish(m)
        if more:
            gather_near(m + 1, far - 1)
    for m in range(items - micro):
        pass_on(m).wait_send()
    for m in range(items):
        core_sum(m).wait_send()
        for k in range(far):
            for j in range(1, near):
                near_sum(m, j, k).wait_send()
            if k > 0:
                far_sum(m, k).wait_send()


def run_layer(tokens_in, side, gain, w_gate, w_up, w_down, count):
    far, near = grid_of(count)
    micro, tokens, features = tokens_in.shape
    items, _, side_width = side.shape
    units = w_gate.shape[1]
    width = features + side_width
    lane_rows = near * far * tokens
    share = features // count
    window = -(-(share + LANES - 1) // LANES) * LANES
    bf16 = jnp.bfloat16
    dma = pltpu.SemaphoreType.DMA
    total_rows = 2 * lane_rows * items
    return pl.pallas_call(
        partial(layer_kernel, count, far, near, window, items // micro),
        out_shape=(
            jax.ShapeDtypeStruct((items, tokens, features), bf16),
            jax.ShapeDtypeStruct((side_width, window), jnp.float32),
        ),
        in_specs=[pl.BlockSpec(memory_space=pltpu.VMEM)] * 3 + [pl.BlockSpec(memory_space=pl.ANY)] * 3,
        out_specs=(pl.BlockSpec(memory_space=pltpu.VMEM),) * 2,
        scratch_shapes=[
            pltpu.VMEM((items, 2 * lane_rows, width), bf16),
            pltpu.VMEM(tokens_in.shape, bf16),
            pltpu.VMEM(w_gate.shape, bf16),
            pltpu.VMEM(w_up.shape, bf16),
            pltpu.VMEM(w_down.shape, bf16),
            pltpu.VMEM((lane_rows, units), bf16),
            pltpu.VMEM((items, lane_rows, features), bf16),
            pltpu.VMEM((items, near - 1, far, tokens, features), bf16),
            pltpu.VMEM((items, far - 1, tokens, features), bf16),
            dma((3,)),
            dma((items, 2 * far)),
            dma((items, near * far)),
            dma((items, near * far)),
            dma((items, count)),
            dma((items,)),
            dma((items,)),
            dma((items, near - 1, far)),
            dma((items, near - 1, far)),
            dma((items, far - 1)),
            dma((items, far - 1)),
            dma((micro,)),
            dma((micro,)),
        ],
        compiler_params=pltpu.CompilerParams(
            collective_id=0, has_side_effects=True, vmem_limit_bytes=60 * 1024 * 1024
        ),
        cost_estimate=pl.CostEstimate(
            flops=6 * total_rows * features * units,
            bytes_accessed=6 * features * units,
            transcendentals=total_rows * units,
        ),
    )(tokens_in, side, gain, w_gate, w_up, w_down)


def side_columns(ids, gates, tangents, count, width):
    named = (ids[..., None] == jnp.arange(count, dtype=jnp.int32)).astype(jnp.float32)
    weight = jnp.sum(gates[..., None] * named, axis=-2)
    high = weight.astype(jnp.bfloat16)
    low = (weight - high.astype(jnp.float32)).astype(jnp.bfloat16)
    side = jnp.concatenate([high, low, tangents], axis=-1)
    return jnp.pad(side, ((0, 0), (0, 0), (0, width - side.shape[-1])))


def on_device(
    down_tokens,
    up_tokens,
    norm_gain,
    w_gate,
    w_up,
    w_down,
    down_ids,
    down_gates,
    up_ids,
    up_gates,
    key_cotangent,
):
    sections = lax.axis_size("pipe")
    section = lax.axis_index("pipe")
    count = lax.axis_size("expert")
    features = down_tokens.shape[-1]
    rope = key_cotangent.shape[-1]
    share = features // count
    side_width = -(-(2 * count + rope) // LANES) * LANES
    window = -(-(share + LANES - 1) // LANES) * LANES
    side_down = side_columns(down_ids[0], down_gates[0], key_cotangent[0, 0], count, side_width)
    side_up = side_columns(up_ids[0], up_gates[0], key_cotangent[0, 1], count, side_width)
    carried = jnp.where(section == 0, down_tokens, up_tokens)
    down_states = jnp.zeros_like(down_tokens)
    up_states = jnp.zeros_like(up_tokens)
    key_grad = 0.0
    micro = down_tokens.shape[0]
    turns = sections if sections == 2 and micro > 1 else 1
    for call in range(0, sections, turns):
        sides = []
        for turn in range(call, call + turns):
            down_on, up_on = section == turn, section == sections - 1 - turn
            side = jnp.where(down_on, side_down, side_up)
            sides.append(jnp.where(down_on | up_on, side, jnp.zeros_like(side)))
        side = jnp.concatenate(sides, axis=0)
        outputs, grad = run_layer(carried, side, norm_gain, w_gate[0, 0], w_up[0, 0], w_down[0, 0], count)
        key_grad = key_grad + grad
        for turn in range(call, call + turns):
            output = outputs[(turn - call) * micro : (turn - call + 1) * micro]
            down_states = jnp.where(section == turn, output, down_states)
            up_states = jnp.where(section == sections - 1 - turn, output, up_states)
        if turn + 1 < sections:
            carried = lax.ppermute(
                output, "pipe", [(turn, turn + 1), (sections - 1 - turn, sections - 2 - turn)]
            )
    first = lax.axis_index("expert") * share
    start = jnp.minimum(first // LANES * LANES, features + side_width - window)
    grad_rows = lax.dynamic_slice(key_grad, (2 * count, first - start), (rope, share)).T
    return (down_states[None], up_states[None], grad_rows[None])


def solution(mesh):
    return jax.shard_map(
        on_device,
        mesh=mesh,
        in_specs=(
            P(None, "expert", None),
            P(None, "expert", None),
            P("pipe", None),
            P("pipe", "expert", None, None),
            P("pipe", "expert", None, None),
            P("pipe", "expert", None, None),
            P("pipe", None, "expert", None),
            P("pipe", None, "expert", None),
            P("pipe", None, "expert", None),
            P("pipe", None, "expert", None),
            P("pipe", None, None, "expert", None),
        ),
        out_specs=(
            P("pipe", None, "expert", None),
            P("pipe", None, "expert", None),
            P("pipe", "expert", None),
        ),
        check_vma=False,
    )
```
